32 devices in a mesh: gx: 4 (over y, x), gy: 8 (over z, core).
Axes of the slice: x: 2, y: 2, z: 4, core: 2. Of those that a mesh axis runs over, the one named last changes fastest.
Arguments:
- traces: bfloat16 [2048, 1024], P(('gx', 'gy')), may hold values from -6 to 6
- filter_taps: float32 [8], replicated, may hold values from -3 to 3
- aperture: int32 [2048, 8], P(('gx', 'gy')), may hold values from 0 to 31, all different within a row; in each aligned block of 64 rows (0 to 63, 64 to 127, ...) at most 32 rows name the same one
- midpoint: int32 [2048, 8], P(('gx', 'gy')), may hold values from 0 to 287
- time_index: int32 [128, 64], replicated, may hold values from 0 to 1022
- time_frac: float32 [128, 64], replicated, may hold values from 0 to 1
- amplitude: float32 [128, 64], replicated, may hold values from 0.02 to 0.2
Outputs:
- image: float32 [16, 4096], P('gx', 'gy')
The draws below stay inside these ranges and needn't reach their ends.
Inputs may be any that keep to these rules, and one draw needn't show every extreme that they name: `aperture`: each trace names 8 different tiles; among the rows of one device no tile is named by more than 32 rows, a bound that some block reaches.
All inputs are finite; a program needn't handle non-finite values.
Results may differ from the reference program's by a relative error of at most 0.005.
Values may be sent and summed in bfloat16 or wider, within the bound.
A program may use at most 64 MiB of HBM per device.

```python
import math
import jax
import jax.numpy as jnp
import numpy as np
from jax import lax

TR_DEV = 64
APER = 8
TX = 4
TY = 8
NT = 1024
Z = 64
TAPS = 8
CAP = 32
TRACES = 2048
NX = 16
NY = 64
DBIN = 128
MBINS = 288
N_GX = 4
N_GY = 8


def with_ends(array, stream_key, low, largest):
    longest = array.shape.index(max(array.shape))
    spots = []
    for shift in (0, 1):
        where = [jax.random.randint(jax.random.fold_in(stream_key, axis), (), 0, length) for axis, length in enumerate(array.shape)]
        where[longest] = (where[longest] + shift) % array.shape[longest]
        spots.append(tuple(where))
    return array.at[spots[0]].set(low).at[spots[1]].set(largest)


def shard_levels(rng, shape, pieces, smallest, largest):
    gain = 1.0
    for position, shards_of in pieces:
        steps = jax.random.uniform(jax.random.fold_in(jax.random.fold_in(rng, 6), position), (shards_of,), jnp.float32, smallest / len(pieces), largest / len(pieces))
        gain = gain * jnp.repeat(jnp.exp(steps), shape[position] // shards_of).reshape((-1,) + (1,) * (len(shape) - 1 - position))
    return gain


def shared_out(key, own, number, rows, number_of, top, reach, slope):
    ranking = jax.random.permutation(key, number_of)
    crowded, ordinary = load_shares(number_of, rows * top, reach, slope, True), load_shares(number_of, rows * top, reach, slope, False)
    places = jnp.arange(number_of)

    def named(sizes, offset_by):
        used = int((sizes > 0).sum())
        fixed = max(1, used // 4)
        passed = fixed + (places - fixed + offset_by * (used - fixed)) % max(1, number_of - fixed)
        return jnp.zeros((number_of,), jnp.int32).at[ranking[jnp.where(places < fixed, places, passed)]].set(jnp.asarray(sizes, jnp.int32))

    sizes = jnp.where(number % 4 == 0, named(crowded, number // 4), named(ordinary, number - number // 4 - 1))
    mixed = jax.random.permutation(jax.random.fold_in(own, 3), number_of)
    giver, sink = mixed[0:number_of // 2 * 2:2], mixed[1:number_of // 2 * 2:2]
    slack = jnp.minimum(sizes[giver] - 1, reach - sizes[sink]) // 2
    slack = jnp.where((giver == ranking[0]) | (sink == ranking[0]) | (sizes[sink] == 0), 0, jnp.maximum(slack, 0))
    passed = jax.random.randint(jax.random.fold_in(own, 4), (number_of // 2,), 0, 1 << 20) % (slack + 1)
    sizes = sizes.at[giver].add(-passed).at[sink].add(passed)
    members = jnp.searchsorted(jnp.cumsum(sizes), jnp.arange(rows * top), side="right").astype(jnp.int32)
    grid = members.reshape(top, rows).T
    grid = grid[jax.random.permutation(jax.random.fold_in(own, 1), rows)]
    offset_by = jax.random.randint(jax.random.fold_in(own, 2), (rows, 1), 0, top)
    return jnp.take_along_axis(grid, (jnp.arange(top)[None, :] + offset_by) % top, axis=1)


def load_shares(amount, total, most, skew, full):
    weights = [(1 << 20) // math.isqrt(grade ** skew) + 1 for grade in range(1, amount + 1)]
    largest = most if full else min(most, max(-(-total // amount), total * weights[0] // sum(weights)))
    least = 1 if total - largest >= amount - 1 else 0
    given, surplus = [largest] + [least] * (amount - 1), total - largest - least * (amount - 1)
    while surplus > 0:
        candidates = [i for i in range(1, amount) if given[i] < largest] or [i for i in range(1, amount) if given[i] < most]
        whole, left = sum([weights[i] for i in candidates]), surplus
        for i in candidates:
            more = min(most - given[i], max(1, left * weights[i] // whole), surplus)
            given[i] = given[i] + more
            surplus = surplus - more
    return np.array(given)


def centred(own_key, extent, scale, bound, shards=(), held_as=jnp.bfloat16):
    result = scale * jax.random.normal(own_key, extent, jnp.float32)
    if shards:
        result = result * shard_levels(own_key, extent, shards, -0.22, 0.18)
    return jnp.clip(result, -bound, bound).astype(held_as)


def setup_inputs(seed: int = 0) -> dict:
    arg_keys = jax.random.split(jax.random.key(seed), 8)
    traces = centred(arg_keys[0], (TRACES, NT), 1.0, 6.0, ((0, 32),))
    filter_taps = centred(arg_keys[1], (TAPS,), 0.35, 3.0, (), jnp.float32)
    aperture_keys = jax.random.split(jax.random.fold_in(arg_keys[2], 1), TRACES // TR_DEV)
    aperture_turns = jax.random.permutation(jax.random.fold_in(arg_keys[2], 3), TRACES // TR_DEV)
    aperture = jax.vmap(lambda own, number: shared_out(jax.random.fold_in(arg_keys[2], 2), own, number, TR_DEV, N_GX * N_GY, APER, CAP, 2))(aperture_keys, aperture_turns).reshape((TRACES, APER))
    midpoint = with_ends(jax.random.randint(arg_keys[3], (TRACES, APER), 0, MBINS), jax.random.fold_in(arg_keys[3], 1), 0, MBINS - 1).astype(jnp.int32)
    time_index = with_ends(jax.random.randint(arg_keys[4], (DBIN, Z), 0, NT - 1), jax.random.fold_in(arg_keys[4], 1), 0, (NT - 1) - 1).astype(jnp.int32)
    time_frac = jnp.clip(jax.random.uniform(arg_keys[5], (DBIN, Z), jnp.float32, 0.0, 1.0), 0.0, 1.0)
    amplitude = jnp.clip(jnp.exp(jax.random.uniform(arg_keys[6], (DBIN, Z), jnp.float32, math.log(0.02), math.log(0.2))), 0.02, 0.2)
    return dict(traces=traces, filter_taps=filter_taps, aperture=aperture, midpoint=midpoint, time_index=time_index, time_frac=time_frac, amplitude=amplitude)


def fir_filter(traces, filter_taps):
    samples = traces.shape[1]
    taps_count = filter_taps.shape[0]
    padded = jnp.pad(traces.astype(jnp.float32), ((0, 0), (taps_count - 1, 0)))
    total = jnp.zeros(traces.shape, jnp.float32)
    for offset in range(taps_count):
        total = total + filter_taps[offset] * padded[:, taps_count - 1 - offset:taps_count - 1 - offset + samples]
    return total.astype(jnp.bfloat16)


def reference(traces, filter_taps, aperture, midpoint, time_index, time_frac, amplitude):
    filtered = fir_filter(traces, filter_taps)
    w_low = (1.0 - time_frac).astype(jnp.bfloat16)
    w_high = time_frac.astype(jnp.bfloat16)
    tile_count = N_GX * N_GY
    per_block = TR_DEV * APER
    points = TX * TY
    across = jnp.arange(points, dtype=jnp.int32) // TY
    along = jnp.arange(points, dtype=jnp.int32) % TY

    def one_block(image, blocks):
        rows, targets, mids = blocks
        owner = jnp.arange(per_block, dtype=jnp.int32) // APER
        trace_rows = rows[owner]
        mid_row = mids // (3 * TY)
        mid_col = mids % (3 * TY)
        bins = jnp.abs(mid_row[:, None] - TX - across[None, :]) * (2 * TY) + jnp.abs(mid_col[:, None] - TY - along[None, :])
        index = time_index[bins].reshape(per_block, points * Z).astype(jnp.int32)
        first = jnp.take_along_axis(trace_rows, index, axis=1).astype(jnp.float32)
        second = jnp.take_along_axis(trace_rows, index + 1, axis=1).astype(jnp.float32)
        value = w_low[bins].reshape(per_block, points * Z).astype(jnp.float32) * first + w_high[bins].reshape(per_block, points * Z).astype(jnp.float32) * second
        scaled = (amplitude[bins].reshape(per_block, points * Z) * value).astype(jnp.bfloat16)
        scaled = lax.optimization_barrier(scaled).astype(jnp.float32)
        image = image + jax.ops.segment_sum(scaled, targets, num_segments=tile_count)
        return image, None

    blocks = (filtered.reshape(tile_count, TR_DEV, NT), aperture.reshape(tile_count, per_block), midpoint.reshape(tile_count, per_block))
    image, _ = lax.scan(one_block, jnp.zeros((tile_count, points * Z), jnp.float32), blocks)
    raw = image.reshape(N_GX, N_GY, TX, TY, Z).transpose(0, 2, 1, 3, 4).reshape(NX, NY, Z)
    padded = jnp.pad(raw, ((1, 1), (1, 1), (0, 0)))
    beside = padded[2:, 1:-1] + padded[:-2, 1:-1] + padded[1:-1, 2:] + padded[1:-1, :-2]
    smooth = raw + 0.25 * beside
    return smooth.reshape(NX, NY * Z)
```

```python
import functools

import jax
import jax.numpy as jnp
from jax import lax
from jax.experimental import pallas as pl
from jax.experimental.pallas import tpu as pltpu
from jax.sharding import PartitionSpec as P

TX = 4
TY = 8
MESH = pl.DeviceIdType.MESH
WINDOW = 256
PAIRS = 14
FLAT = 32
STRIDE = PAIRS * FLAT


def local_kernel(
    ngx, ngy, taps_ref, ap_ref, mid_ref, tr_ref, ti_ref, tf_ref, am_ref, out_ref,
    f4_ref, idx_ref, low_ref, high_ref, amp_ref, tab_ref, img_ref,
):
    f32, bf16 = jnp.float32, jnp.bfloat16
    rows, samples = tr_ref.shape
    taps_count = taps_ref.shape[0]
    entries = ap_ref.shape[1]
    windows = samples // WINDOW
    span = 2 * TY
    cols = idx_ref.shape[1]
    pitch = ngy * TY + 16

    x = tr_ref[...].astype(f32)
    lane = lax.broadcasted_iota(jnp.int32, (rows, samples), 1)
    total = jnp.zeros((rows, samples), f32)
    for k in range(taps_count):
        moved = x if k == 0 else jnp.where(lane < k, 0.0, pltpu.roll(x, k, 1))
        total = total + taps_ref[k] * moved
    filtered = total.astype(bf16)
    for j in range(windows):
        f4_ref[j * rows : (j + 1) * rows, :] = filtered[:, j * WINDOW : (j + 1) * WINDOW]
    rounded = filtered.astype(f32)
    edges = [rounded[:, j * WINDOW : j * WINDOW + 1] for j in range(1, windows)]

    for m in range(TX):
        def side(ref):
            return jnp.concatenate(
                [ref[(2 * m) * span : (2 * m + 1) * span, :], ref[(2 * m + 1) * span : (2 * m + 2) * span, :]],
                axis=1,
            )

        here = slice(m * 128, (m + 1) * 128)
        frac = side(tf_ref)
        idx_ref[:, here] = side(ti_ref)
        low_ref[:, here] = (1.0 - frac).astype(bf16).astype(f32)
        high_ref[:, here] = frac.astype(bf16).astype(f32)
        amp_ref[:, here] = side(am_ref)

    first = lax.broadcasted_iota(jnp.int32, (rows, 128), 1) < 64

    def per_distance(b, carry):
        idx = idx_ref[pl.ds(b, 1), :]
        low = low_ref[pl.ds(b, 1), :]
        high = high_ref[pl.ds(b, 1), :]
        amp = amp_ref[pl.ds(b, 1), :]
        inside = idx & (WINDOW - 1)
        window = idx >> 8
        q = jnp.broadcast_to(inside.astype(f32), (16, cols)).astype(bf16)
        lowb = jnp.broadcast_to(low, (16, cols)).astype(bf16)
        highb = jnp.broadcast_to(high, (16, cols)).astype(bf16)
        q1 = q + jnp.ones((), bf16)
        at = lax.broadcasted_iota(jnp.int32, (16, cols), 0).astype(f32).astype(bf16)
        zero = jnp.zeros((16, cols), bf16)
        blocks = []
        for i in range(WINDOW // 16):
            here = at + jnp.asarray(16 * i, bf16)
            blocks.append(jnp.where(here == q, lowb, jnp.where(here == q1, highb, zero)))
        weights = jnp.concatenate(blocks, axis=0)
        products = jnp.dot(f4_ref[...], weights, preferred_element_type=f32)
        over = jnp.where(inside == WINDOW - 1, high, 0.0)
        value = products[(windows - 1) * rows :]
        edge = jnp.broadcast_to(edges[windows - 2], (rows, cols))
        for j in range(windows - 2, -1, -1):
            value = jnp.where(window == j, products[j * rows : (j + 1) * rows], value)
            if j < windows - 2:
                edge = jnp.where(window == j, jnp.broadcast_to(edges[j], (rows, cols)), edge)
        value = value + over * edge
        sample = (amp * value).astype(bf16).astype(f32)
        own = [sample[:, m * 128 : (m + 1) * 128] for m in range(TX)]
        swapped = [pltpu.roll(s, 64, 1) for s in own]

        def put(offset, block):
            start = (offset + 6) * FLAT + 15
            tab_ref[pl.ds(start - b, rows, stride=STRIDE), :] = block
            tab_ref[pl.ds(start + b, rows, stride=STRIDE), :] = block

        for m in range(TX):
            put(2 * m + 1, swapped[m])
            put(-2 * m, own[m])
            if m < TX - 1:
                put(2 * m + 2, jnp.where(first, own[m + 1], own[m]))
                put(-2 * m - 1, jnp.where(first, swapped[m], swapped[m + 1]))
        return carry

    lax.fori_loop(0, span, per_distance, 0)

    img_ref[...] = jnp.zeros_like(img_ref)

    def per_trace(t, carry):
        base = t * STRIDE + 23
        source, place = [], []
        for e in range(entries):
            m = mid_ref[t, e]
            tile = ap_ref[t, e]
            source.append(base - m + 56 * ((m * 2731) >> 16))
            place.append(
                pl.multiple_of(pitch + 8 + (tile // ngy) * (2 * pitch) + (tile % ngy) * TY, 8)
            )
        sums = []
        for e in range(entries):
            sums.append(img_ref[pl.ds(place[e], TY), :] + tab_ref[pl.ds(source[e] + 2 * FLAT, TY), :])
            sums.append(img_ref[pl.ds(place[e] + pitch, TY), :] + tab_ref[pl.ds(source[e], TY), :])
        for e in range(entries):
            img_ref[pl.ds(place[e], TY), :] = sums[2 * e]
            img_ref[pl.ds(place[e] + pitch, TY), :] = sums[2 * e + 1]
        return carry

    lax.fori_loop(0, rows, per_trace, 0)

    head = lax.broadcasted_iota(jnp.int32, (TY, 128), 1) < 64

    def per_tile(tile, carry):
        start = pl.multiple_of(pitch + 8 + (tile // ngy) * (2 * pitch) + (tile % ngy) * TY, 8)
        planes = [img_ref[pl.ds(start + (p - 1) * pitch, TY), :] for p in range(4)]
        parts = []
        for u in range(2):
            below, mid, above = planes[u], planes[u + 1], planes[u + 2]
            along = img_ref[pl.ds(start + u * pitch - 1, TY), :] + img_ref[pl.ds(start + u * pitch + 1, TY), :]
            across = pltpu.roll(jnp.where(head, above + mid, mid + below), 64, 1)
            parts.append(mid + 0.25 * (across + along))
        out_ref[tile] = jnp.concatenate(parts, axis=0).astype(bf16)
        return carry

    lax.fori_loop(0, ngx * ngy, per_tile, 0, unroll=4)


def exchange_kernel(count, ngy, part_ref, out_ref, held, send_sem, recv_sem):
    me = lax.axis_index("gx") * ngy + lax.axis_index("gy")

    def at(peer):
        return (peer // ngy, peer % ngy)

    barrier = pltpu.get_barrier_semaphore()

    def greet(step, carry):
        pl.semaphore_signal(barrier, inc=1, device_id=at((me + step) % count), device_id_type=MESH)
        return carry

    lax.fori_loop(1, count, greet, 0)
    pl.semaphore_wait(barrier, count - 1)

    def copy(step):
        peer = (me + step) % count
        return pltpu.make_async_remote_copy(
            src_ref=part_ref.at[peer],
            dst_ref=held.at[step],
            send_sem=send_sem.at[step],
            recv_sem=recv_sem.at[step],
            device_id=at(peer),
            device_id_type=MESH,
        )

    def send(step, carry):
        copy(step).start()
        return carry

    lax.fori_loop(1, count, send, 0)

    def take(step, total):
        copy(step).wait_recv()
        return total + held[step].astype(jnp.float32)

    total = lax.fori_loop(1, count, take, part_ref[me].astype(jnp.float32))
    out_ref[...] = total

    def done(step, carry):
        copy(step).wait_send()
        return carry

    lax.fori_loop(1, count, done, 0)


def body(ngx, ngy, traces, filter_taps, aperture, midpoint, time_index, time_frac, amplitude):
    rows, samples = traces.shape
    depth = time_frac.shape[1]
    count = ngx * ngy
    span = 2 * TY
    cols = 2 * TX * depth
    vmem = pl.BlockSpec(memory_space=pltpu.VMEM)
    smem = pl.BlockSpec(memory_space=pltpu.SMEM)
    parts = pl.pallas_call(
        functools.partial(local_kernel, ngx, ngy),
        out_shape=jax.ShapeDtypeStruct((count, 2 * TY, 2 * depth), jnp.bfloat16),
        in_specs=[smem, smem, smem, vmem, vmem, vmem, vmem],
        out_specs=vmem,
        scratch_shapes=[
            pltpu.VMEM((rows * samples // WINDOW, WINDOW), jnp.bfloat16),
            pltpu.VMEM((span, cols), jnp.int32),
            pltpu.VMEM((span, cols), jnp.float32),
            pltpu.VMEM((span, cols), jnp.float32),
            pltpu.VMEM((span, cols), jnp.float32),
            pltpu.VMEM((rows * STRIDE, 2 * depth), jnp.float32),
            pltpu.VMEM(((2 * ngx + 2) * (ngy * TY + 16), 2 * depth), jnp.float32),
        ],
        compiler_params=pltpu.CompilerParams(vmem_limit_bytes=40 * 1024 * 1024),
        name="migrate",
    )(filter_taps, aperture, midpoint, traces, time_index, time_frac, amplitude)
    image = pl.pallas_call(
        functools.partial(exchange_kernel, count, ngy),
        out_shape=jax.ShapeDtypeStruct((2 * TY, 2 * depth), jnp.float32),
        in_specs=[vmem],
        out_specs=vmem,
        scratch_shapes=[
            pltpu.VMEM((count, 2 * TY, 2 * depth), jnp.bfloat16),
            pltpu.SemaphoreType.DMA((count,)),
            pltpu.SemaphoreType.DMA((count,)),
        ],
        compiler_params=pltpu.CompilerParams(collective_id=0, has_side_effects=True),
        name="exchange",
    )(parts)
    return image.reshape(2, TY, 2, depth).transpose(0, 2, 1, 3).reshape(TX, TY * depth)


def solution(mesh):
    in_specs = (
        P(("gx", "gy"), None),
        P(),
        P(("gx", "gy"), None),
        P(("gx", "gy"), None),
        P(),
        P(),
        P(),
    )
    return jax.shard_map(
        functools.partial(body, mesh.shape["gx"], mesh.shape["gy"]),
        mesh=mesh,
        in_specs=in_specs,
        out_specs=P("gx", "gy"),
        check_vma=False,
    )
```

```python
import functools

import jax
import jax.numpy as jnp
from jax import lax
from jax.experimental import pallas as pl
from jax.experimental.pallas import tpu as pltpu
from jax.sharding import PartitionSpec as P

TX = 4
TY = 8
MESH = pl.DeviceIdType.MESH
WINDOW = 256
PAIRS = 7
FLAT = 32
PITCH = 72


def local_kernel(
    ngx, ngy, taps_hbm, ap_hbm, mid_hbm, tr_hbm, ti_hbm, tf_hbm, am_hbm, out_ref,
    taps_ref, ap_ref, mid_ref, tr_ref, ti_ref, tf_ref, am_ref, arrive,
    f4_ref, idx_ref, low_ref, high_ref, amp_ref, tab_ref, one_ref, two_ref, img_ref,
    where_ref, spots_ref, moved_sem,
):
    f32, bf16 = jnp.float32, jnp.bfloat16
    rows, samples = tr_ref.shape
    taps_count = taps_ref.shape[0]
    entries = ap_ref.shape[0]
    windows = samples // WINDOW
    span = 2 * TY
    cols = idx_ref.shape[1]
    pitch = ngy * TY + 16
    tiles = ngx * ngy

    pairs = [
        (ap_hbm, ap_ref), (mid_hbm, mid_ref), (taps_hbm, taps_ref), (tr_hbm, tr_ref),
        (ti_hbm, ti_ref), (tf_hbm, tf_ref), (am_hbm, am_ref),
    ]
    copies = [pltpu.make_async_copy(a, b, arrive.at[i]) for i, (a, b) in enumerate(pairs)]
    for c in copies:
        c.start()
    one_ref[...] = jnp.zeros_like(one_ref)
    two_ref[...] = jnp.zeros_like(two_ref)
    img_ref[...] = jnp.zeros_like(img_ref)

    copies[0].wait()
    copies[1].wait()
    mids = mid_ref[...]
    tile = ap_ref[...]
    row = (mids * 2731) >> 16
    base = 23 - mids + 24 * row
    for u in range(2):
        apart = row - 4 - 2 * u
        near = jnp.maximum(apart, 1 - apart) - 1
        bank = jnp.where(apart <= 0, 1, 0)
        where_ref[(2 * u) * entries : (2 * u + 1) * entries, 0:rows] = (near * FLAT + base) * PITCH
        where_ref[(2 * u + 1) * entries : (2 * u + 2) * entries, 0:rows] = (tile * 4 + bank * 2 + u) * TY
    moving = pltpu.make_async_copy(where_ref, spots_ref, moved_sem)
    moving.start()

    copies[2].wait()
    copies[3].wait()
    x = tr_ref[...].astype(f32)
    lane = lax.broadcasted_iota(jnp.int32, (rows, samples), 1)
    total = jnp.zeros((rows, samples), f32)
    for k in range(taps_count):
        moved = x if k == 0 else jnp.where(lane < k, 0.0, pltpu.roll(x, k, 1))
        total = total + taps_ref[k] * moved
    filtered = total.astype(bf16)
    for j in range(windows):
        f4_ref[j * rows : (j + 1) * rows, :] = filtered[:, j * WINDOW : (j + 1) * WINDOW]
    rounded = filtered.astype(f32)
    edges = [rounded[:, j * WINDOW : j * WINDOW + 1] for j in range(1, windows)]

    for c in copies[4:]:
        c.wait()
    for m in range(TX):
        def side(ref):
            both = ref[:, (2 * m) * span : (2 * m + 2) * span].T
            return jnp.concatenate([both[:span], both[span:]], axis=1)

        here = slice(m * 128, (m + 1) * 128)
        frac = side(tf_ref)
        idx_ref[:, here] = side(ti_ref)
        low_ref[:, here] = (1.0 - frac).astype(bf16).astype(f32)
        high_ref[:, here] = frac.astype(bf16).astype(f32)
        amp_ref[:, here] = side(am_ref)

    first = lax.broadcasted_iota(jnp.int32, (rows, 128), 1) < 64

    def per_distance(b, carry):
        idx = idx_ref[pl.ds(b, 1), :]
        low = low_ref[pl.ds(b, 1), :]
        high = high_ref[pl.ds(b, 1), :]
        amp = amp_ref[pl.ds(b, 1), :]
        inside = idx & (WINDOW - 1)
        window = idx >> 8
        q = jnp.broadcast_to(inside.astype(f32), (16, cols)).astype(bf16)
        lowb = jnp.broadcast_to(low, (16, cols)).astype(bf16)
        highb = jnp.broadcast_to(high, (16, cols)).astype(bf16)
        q1 = q + jnp.ones((), bf16)
        at = lax.broadcasted_iota(jnp.int32, (16, cols), 0).astype(f32).astype(bf16)
        zero = jnp.zeros((16, cols), bf16)
        blocks = []
        for i in range(WINDOW // 16):
            here = at + jnp.asarray(16 * i, bf16)
            blocks.append(jnp.where(here == q, lowb, jnp.where(here == q1, highb, zero)))
        weights = jnp.concatenate(blocks, axis=0)
        products = jnp.dot(f4_ref[...], weights, preferred_element_type=f32)
        over = jnp.where(inside == WINDOW - 1, high, 0.0)
        value = products[(windows - 1) * rows :]
        edge = jnp.broadcast_to(edges[windows - 2], (rows, cols))
        for j in range(windows - 2, -1, -1):
            value = jnp.where(window == j, products[j * rows : (j + 1) * rows], value)
            if j < windows - 2:
                edge = jnp.where(window == j, jnp.broadcast_to(edges[j], (rows, cols)), edge)
        value = value + over * edge
        sample = (amp * value).astype(bf16).astype(f32)
        own = [sample[:, m * 128 : (m + 1) * 128] for m in range(TX)]

        def put(far, block):
            start = (far - 1) * FLAT + 15
            tab_ref[pl.ds(pl.multiple_of((start - b) * PITCH, 8), rows), :] = block
            tab_ref[pl.ds(pl.multiple_of((start + b) * PITCH, 8), rows), :] = block

        for m in range(TX):
            put(2 * m + 1, pltpu.roll(own[m], 64, 1))
            if m < TX - 1:
                put(2 * m + 2, jnp.where(first, own[m + 1], own[m]))
        return carry

    lax.fori_loop(0, span, per_distance, 0, unroll=16)

    moving.wait()
    half = rows // 2

    def per_trace(t, carry):
        for into, trace in ((one_ref, t), (two_ref, t + half)):
            sums = []
            for e in range(entries):
                for u in range(2):
                    source = spots_ref[(2 * u) * entries + e, trace] + trace
                    place = pl.multiple_of(spots_ref[(2 * u + 1) * entries + e, trace], TY)
                    sums.append(
                        (place, into[pl.ds(place, TY), :] + tab_ref[pl.ds(source, TY, stride=PITCH), :])
                    )
            for place, value in sums:
                into[pl.ds(place, TY), :] = value
        return carry

    lax.fori_loop(0, half, per_trace, 0)

    def gather(tile, carry):
        spot = pl.multiple_of(pitch + 8 + (tile // ngy) * (2 * pitch) + (tile % ngy) * TY, 8)
        for u in range(2):
            plain = pl.multiple_of((tile * 4 + u) * TY, TY)
            turned = pl.multiple_of((tile * 4 + 2 + u) * TY, TY)
            img_ref[pl.ds(spot + u * pitch, TY), :] = (
                one_ref[pl.ds(plain, TY), :] + two_ref[pl.ds(plain, TY), :]
            ) + pltpu.roll(one_ref[pl.ds(turned, TY), :] + two_ref[pl.ds(turned, TY), :], 64, 1)
        return carry

    lax.fori_loop(0, tiles, gather, 0, unroll=8)

    head = lax.broadcasted_iota(jnp.int32, (TY, 128), 1) < 64

    def per_tile(tile, carry):
        start = pl.multiple_of(pitch + 8 + (tile // ngy) * (2 * pitch) + (tile % ngy) * TY, 8)
        planes = [img_ref[pl.ds(start + (p - 1) * pitch, TY), :] for p in range(4)]
        parts = []
        for u in range(2):
            below, mid, above = planes[u], planes[u + 1], planes[u + 2]
            along = img_ref[pl.ds(start + u * pitch - 1, TY), :] + img_ref[pl.ds(start + u * pitch + 1, TY), :]
            across = pltpu.roll(jnp.where(head, above + mid, mid + below), 64, 1)
            parts.append(mid + 0.25 * (across + along))
        out_ref[tile] = jnp.concatenate(parts, axis=0).astype(bf16)
        return carry

    lax.fori_loop(0, tiles, per_tile, 0, unroll=8)


def exchange_kernel(count, ngy, part_ref, out_ref, held, send_sem, recv_sem, own_sem):
    me = lax.axis_index("gx") * ngy + lax.axis_index("gy")

    def at(peer):
        return (peer // ngy, peer % ngy)

    barrier = pltpu.get_barrier_semaphore()

    def greet(step, carry):
        pl.semaphore_signal(barrier, inc=1, device_id=at((me + step) % count), device_id_type=MESH)
        return carry

    lax.fori_loop(1, count, greet, 0)
    pl.semaphore_wait(barrier, count - 1)

    def copy(step):
        peer = (me + step) % count
        return pltpu.make_async_remote_copy(
            src_ref=part_ref.at[peer],
            dst_ref=held.at[step],
            send_sem=send_sem.at[step],
            recv_sem=recv_sem.at[step],
            device_id=at(peer),
            device_id_type=MESH,
        )

    def send(step, carry):
        copy(step).start()
        return carry

    lax.fori_loop(1, count, send, 0)
    mine = pltpu.make_async_copy(part_ref.at[me], held.at[0], own_sem)
    mine.start()
    mine.wait()

    def take(step, total):
        copy(step).wait_recv()
        return total + held[step].astype(jnp.float32)

    total = lax.fori_loop(1, count, take, held[0].astype(jnp.float32))
    out_ref[...] = total

    def done(step, carry):
        copy(step).wait_send()
        return carry

    lax.fori_loop(1, count, done, 0)


def body(ngx, ngy, traces, filter_taps, aperture, midpoint, time_index, time_frac, amplitude):
    rows, samples = traces.shape
    depth = time_frac.shape[1]
    count = ngx * ngy
    span = 2 * TY
    cols = 2 * TX * depth
    vmem = pl.BlockSpec(memory_space=pltpu.VMEM)
    hbm = pl.BlockSpec(memory_space=pltpu.HBM)
    entries = aperture.shape[1]
    i32, f32, bf16 = jnp.int32, jnp.float32, jnp.bfloat16
    parts = pl.pallas_call(
        functools.partial(local_kernel, ngx, ngy),
        out_shape=jax.ShapeDtypeStruct((count, 2 * TY, 2 * depth), jnp.bfloat16),
        in_specs=[hbm] * 7,
        out_specs=vmem,
        scratch_shapes=[
            pltpu.SMEM(filter_taps.shape, f32),
            pltpu.VMEM((entries, rows), i32),
            pltpu.VMEM((entries, rows), i32),
            pltpu.VMEM((rows, samples), bf16),
            pltpu.VMEM(time_index.shape[::-1], i32),
            pltpu.VMEM(time_index.shape[::-1], f32),
            pltpu.VMEM(time_index.shape[::-1], f32),
            pltpu.SemaphoreType.DMA((7,)),
            pltpu.VMEM((rows * samples // WINDOW, WINDOW), bf16),
            pltpu.VMEM((span, cols), i32),
            pltpu.VMEM((span, cols), f32),
            pltpu.VMEM((span, cols), f32),
            pltpu.VMEM((span, cols), f32),
            pltpu.VMEM((PAIRS * FLAT * PITCH, 2 * depth), f32),
            pltpu.VMEM((count * 4 * TY, 2 * depth), f32),
            pltpu.VMEM((count * 4 * TY, 2 * depth), f32),
            pltpu.VMEM(((2 * ngx + 2) * (ngy * TY + 16), 2 * depth), f32),
            pltpu.VMEM((4 * entries, 128), i32),
            pltpu.SMEM((4 * entries, 128), i32),
            pltpu.SemaphoreType.DMA,
        ],
        compiler_params=pltpu.CompilerParams(vmem_limit_bytes=40 * 1024 * 1024),
        name="migrate",
    )(filter_taps, aperture.T, midpoint.T, traces, time_index.T, time_frac.T, amplitude.T)
    image = pl.pallas_call(
        functools.partial(exchange_kernel, count, ngy),
        out_shape=jax.ShapeDtypeStruct((2 * TY, 2 * depth), jnp.float32),
        in_specs=[pl.BlockSpec(memory_space=pl.ANY)],
        out_specs=vmem,
        scratch_shapes=[
            pltpu.VMEM((count, 2 * TY, 2 * depth), jnp.bfloat16),
            pltpu.SemaphoreType.DMA((count,)),
            pltpu.SemaphoreType.DMA((count,)),
            pltpu.SemaphoreType.DMA,
        ],
        compiler_params=pltpu.CompilerParams(collective_id=0, has_side_effects=True),
        name="exchange",
    )(parts)
    return image.reshape(2, TY, 2, depth).transpose(0, 2, 1, 3).reshape(TX, TY * depth)


def solution(mesh):
    in_specs = (
        P(("gx", "gy"), None),
        P(),
        P(("gx", "gy"), None),
        P(("gx", "gy"), None),
        P(),
        P(),
        P(),
    )
    return jax.shard_map(
        functools.partial(body, mesh.shape["gx"], mesh.shape["gy"]),
        mesh=mesh,
        in_specs=in_specs,
        out_specs=P("gx", "gy"),
        check_vma=False,
    )
```

```python
import functools

import jax
import jax.numpy as jnp
from jax import lax
from jax.experimental import pallas as pl
from jax.experimental.pallas import tpu as pltpu
from jax.sharding import PartitionSpec as P

TX = 4
LIMIT1 = 63 * 1024 * 1024
LIMIT2 = 16 * 1024 * 1024
TY = 8
MESH = pl.DeviceIdType.MESH
WINDOW = 256
PAIRS = 7
FLAT = 32
PITCH = 8


def local_kernel(
    ngx, ngy, taps_hbm, ap_hbm, mid_hbm, tr_hbm, ti_hbm, tf_hbm, am_hbm, out_ref,
    taps_ref, ap_ref, mid_ref, tr_ref, ti_ref, tf_ref, am_ref, arrive,
    f4_ref, idx_ref, low_ref, high_ref, amp_ref, tab_ref, one_ref, two_ref, img_ref,
    where_ref, spots_ref, moved_sem,
):
    f32, bf16 = jnp.float32, jnp.bfloat16
    rows, samples = tr_ref.shape
    taps_count = taps_ref.shape[0]
    entries = ap_ref.shape[0]
    windows = samples // WINDOW
    span = 2 * TY
    cols = idx_ref.shape[1]
    pitch = ngy * TY + 16
    tiles = ngx * ngy

    pairs = [
        (ap_hbm, ap_ref), (mid_hbm, mid_ref), (taps_hbm, taps_ref), (tr_hbm, tr_ref),
        (ti_hbm, ti_ref), (tf_hbm, tf_ref), (am_hbm, am_ref),
    ]
    copies = [pltpu.make_async_copy(a, b, arrive.at[i]) for i, (a, b) in enumerate(pairs)]
    for c in copies:
        c.start()
    one_ref[...] = jnp.zeros_like(one_ref)
    two_ref[...] = jnp.zeros_like(two_ref)
    img_ref[...] = jnp.zeros_like(img_ref)

    copies[0].wait()
    copies[1].wait()
    mids = mid_ref[...]
    tile = ap_ref[...]
    row = (mids * 2731) >> 16
    base = 23 - mids + 24 * row
    trace = lax.broadcasted_iota(jnp.int32, (entries, rows), 1)
    for u in range(2):
        apart = row - 4 - 2 * u
        near = jnp.maximum(apart, 1 - apart) - 1
        bank = jnp.where(apart <= 0, 1, 0)
        where_ref[(2 * u) * entries : (2 * u + 1) * entries, 0:rows] = (
            (near * (rows // 8) + (trace >> 3)) * FLAT + base
        ) * PITCH + (trace & 7)
        where_ref[(2 * u + 1) * entries : (2 * u + 2) * entries, 0:rows] = (tile * 4 + bank * 2 + u) * TY
    moving = pltpu.make_async_copy(where_ref, spots_ref, moved_sem)
    moving.start()

    copies[2].wait()
    copies[3].wait()
    x = tr_ref[...].astype(f32)
    lane = lax.broadcasted_iota(jnp.int32, (rows, samples), 1)
    total = jnp.zeros((rows, samples), f32)
    for k in range(taps_count):
        moved = x if k == 0 else jnp.where(lane < k, 0.0, pltpu.roll(x, k, 1))
        total = total + taps_ref[k] * moved
    filtered = total.astype(bf16)
    for j in range(windows):
        f4_ref[j * rows : (j + 1) * rows, :] = filtered[:, j * WINDOW : (j + 1) * WINDOW]
    rounded = filtered.astype(f32)
    edges = [rounded[:, j * WINDOW : j * WINDOW + 1] for j in range(1, windows)]

    for c in copies[4:]:
        c.wait()
    for m in range(TX):
        def side(ref):
            both = ref[:, (2 * m) * span : (2 * m + 2) * span].T
            return jnp.concatenate([both[:span], both[span:]], axis=1)

        here = slice(m * 128, (m + 1) * 128)
        frac = side(tf_ref)
        idx_ref[:, here] = side(ti_ref)
        low_ref[:, here] = (1.0 - frac).astype(bf16).astype(f32)
        high_ref[:, here] = frac.astype(bf16).astype(f32)
        amp_ref[:, here] = side(am_ref)

    first = lax.broadcasted_iota(jnp.int32, (rows, 128), 1) < 64

    def per_distance(b, carry):
        idx = idx_ref[pl.ds(b, 1), :]
        low = low_ref[pl.ds(b, 1), :]
        high = high_ref[pl.ds(b, 1), :]
        amp = amp_ref[pl.ds(b, 1), :]
        inside = idx & (WINDOW - 1)
        window = idx >> 8
        q = jnp.broadcast_to(inside.astype(f32), (16, cols)).astype(bf16)
        lowb = jnp.broadcast_to(low, (16, cols)).astype(bf16)
        highb = jnp.broadcast_to(high, (16, cols)).astype(bf16)
        q1 = q + jnp.ones((), bf16)
        at = lax.broadcasted_iota(jnp.int32, (16, cols), 0).astype(f32).astype(bf16)
        zero = jnp.zeros((16, cols), bf16)
        blocks = []
        for i in range(WINDOW // 16):
            here = at + jnp.asarray(16 * i, bf16)
            blocks.append(jnp.where(here == q, lowb, jnp.where(here == q1, highb, zero)))
        weights = jnp.concatenate(blocks, axis=0)
        products = jnp.dot(f4_ref[...], weights, preferred_element_type=f32)
        over = jnp.where(inside == WINDOW - 1, high, 0.0)
        value = products[(windows - 1) * rows :]
        edge = jnp.broadcast_to(edges[windows - 2], (rows, cols))
        for j in range(windows - 2, -1, -1):
            value = jnp.where(window == j, products[j * rows : (j + 1) * rows], value)
            if j < windows - 2:
                edge = jnp.where(window == j, jnp.broadcast_to(edges[j], (rows, cols)), edge)
        value = value + over * edge
        sample = (amp * value).astype(bf16).astype(f32)
        own = [sample[:, m * 128 : (m + 1) * 128] for m in range(TX)]

        def put(far, block):
            for g in range(rows // 8):
                start = ((far - 1) * (rows // 8) + g) * FLAT + 15
                part = block[8 * g : 8 * g + 8]
                tab_ref[pl.ds((start - b) * PITCH, 8), :] = part
                tab_ref[pl.ds((start + b) * PITCH, 8), :] = part

        for m in range(TX):
            put(2 * m + 1, pltpu.roll(own[m], 64, 1))
            if m < TX - 1:
                put(2 * m + 2, jnp.where(first, own[m + 1], own[m]))
        return carry

    lax.fori_loop(0, span, per_distance, 0, unroll=16)

    moving.wait()
    half = rows // 2

    def per_trace(t, carry):
        for into, trace in ((one_ref, t), (two_ref, t + half)):
            sums = []
            for e in range(entries):
                for u in range(2):
                    source = spots_ref[(2 * u) * entries + e, trace]
                    place = pl.multiple_of(spots_ref[(2 * u + 1) * entries + e, trace], TY)
                    sums.append(
                        (place, into[pl.ds(place, TY), :] + tab_ref[pl.ds(source, TY, stride=PITCH), :])
                    )
            for place, value in sums:
                into[pl.ds(place, TY), :] = value
        return carry

    lax.fori_loop(0, half, per_trace, 0)

    def gather(tile, carry):
        spot = pl.multiple_of(pitch + 8 + (tile // ngy) * (2 * pitch) + (tile % ngy) * TY, 8)
        for u in range(2):
            plain = pl.multiple_of((tile * 4 + u) * TY, TY)
            turned = pl.multiple_of((tile * 4 + 2 + u) * TY, TY)
            img_ref[pl.ds(spot + u * pitch, TY), :] = (
                one_ref[pl.ds(plain, TY), :] + two_ref[pl.ds(plain, TY), :]
            ) + pltpu.roll(one_ref[pl.ds(turned, TY), :] + two_ref[pl.ds(turned, TY), :], 64, 1)
        return carry

    lax.fori_loop(0, tiles, gather, 0, unroll=8)

    head = lax.broadcasted_iota(jnp.int32, (TY, 128), 1) < 64

    def per_tile(tile, carry):
        start = pl.multiple_of(pitch + 8 + (tile // ngy) * (2 * pitch) + (tile % ngy) * TY, 8)
        planes = [img_ref[pl.ds(start + (p - 1) * pitch, TY), :] for p in range(4)]
        parts = []
        for u in range(2):
            below, mid, above = planes[u], planes[u + 1], planes[u + 2]
            along = img_ref[pl.ds(start + u * pitch - 1, TY), :] + img_ref[pl.ds(start + u * pitch + 1, TY), :]
            across = pltpu.roll(jnp.where(head, above + mid, mid + below), 64, 1)
            parts.append(mid + 0.25 * (across + along))
        a, b = tile // ngy, tile % ngy
        out_ref[b % 2, a * (ngy // 2) + b // 2] = jnp.concatenate(parts, axis=0).astype(bf16)
        return carry

    lax.fori_loop(0, tiles, per_tile, 0, unroll=8)


def exchange_kernel(
    half, part_ref, out_ref, own, near, both, held, own_sem, near_send, near_recv, send_sem, recv_sem
):
    x, y = lax.axis_index("gx"), lax.axis_index("gy")
    cross = lax.axis_size("gy") // 2
    core = y % 2
    spot = x * cross + y // 2
    twin = (x, y + 1 - 2 * core)

    def at(step):
        peer = (spot + step) % half
        return (peer // cross, (peer % cross) * 2 + core)

    barrier = pltpu.get_barrier_semaphore()
    pl.semaphore_signal(barrier, inc=1, device_id=twin, device_id_type=MESH)

    def greet(step, carry):
        pl.semaphore_signal(barrier, inc=1, device_id=at(step), device_id_type=MESH)
        return carry

    lax.fori_loop(1, half, greet, 0, unroll=True)
    mine = pltpu.make_async_copy(part_ref.at[core], own, own_sem)
    mine.start()
    pl.semaphore_wait(barrier, half)

    swap = pltpu.make_async_remote_copy(
        src_ref=part_ref.at[1 - core],
        dst_ref=near,
        send_sem=near_send,
        recv_sem=near_recv,
        device_id=twin,
        device_id_type=MESH,
    )
    swap.start()
    mine.wait()
    swap.wait_recv()

    def summed(step):
        peer = (spot + step) % half
        return own[peer].astype(jnp.float32) + near[peer].astype(jnp.float32)

    def copy(step):
        return pltpu.make_async_remote_copy(
            src_ref=both.at[step],
            dst_ref=held.at[step],
            send_sem=send_sem.at[step],
            recv_sem=recv_sem.at[step],
            device_id=at(step),
            device_id_type=MESH,
        )

    def send(step, carry):
        both[step] = summed(step).astype(jnp.bfloat16)
        copy(step).start()
        return carry

    lax.fori_loop(1, half, send, 0, unroll=True)

    def take(step, total):
        copy(step).wait_recv()
        return total + held[step].astype(jnp.float32)

    total = lax.fori_loop(1, half, take, summed(0), unroll=True)
    first = lax.broadcasted_iota(jnp.int32, (1, 128), 1) < 64
    turned = pltpu.roll(total, 64, 1)
    for u in range(2):
        for w in range(TY // 2):
            even = slice(u * TY + 2 * w, u * TY + 2 * w + 1)
            odd = slice(u * TY + 2 * w + 1, u * TY + 2 * w + 2)
            here = slice(w * 128, (w + 1) * 128)
            out_ref[2 * u : 2 * u + 1, here] = jnp.where(first, total[even], turned[odd])
            out_ref[2 * u + 1 : 2 * u + 2, here] = jnp.where(first, turned[even], total[odd])

    swap.wait_send()

    def done(step, carry):
        copy(step).wait_send()
        return carry

    lax.fori_loop(1, half, done, 0, unroll=True)


def body(ngx, ngy, traces, filter_taps, aperture, midpoint, time_index, time_frac, amplitude):
    rows, samples = traces.shape
    depth = time_frac.shape[1]
    count = ngx * ngy
    span = 2 * TY
    cols = 2 * TX * depth
    vmem = pl.BlockSpec(memory_space=pltpu.VMEM)
    hbm = pl.BlockSpec(memory_space=pltpu.HBM)
    entries = aperture.shape[1]
    i32, f32, bf16 = jnp.int32, jnp.float32, jnp.bfloat16
    parts = pl.pallas_call(
        functools.partial(local_kernel, ngx, ngy),
        out_shape=jax.ShapeDtypeStruct((2, count // 2, 2 * TY, 2 * depth), jnp.bfloat16),
        in_specs=[hbm] * 7,
        out_specs=vmem,
        scratch_shapes=[
            pltpu.SMEM(filter_taps.shape, f32),
            pltpu.VMEM((entries, rows), i32),
            pltpu.VMEM((entries, rows), i32),
            pltpu.VMEM((rows, samples), bf16),
            pltpu.VMEM(time_index.shape[::-1], i32),
            pltpu.VMEM(time_index.shape[::-1], f32),
            pltpu.VMEM(time_index.shape[::-1], f32),
            pltpu.SemaphoreType.DMA((7,)),
            pltpu.VMEM((rows * samples // WINDOW, WINDOW), bf16),
            pltpu.VMEM((span, cols), i32),
            pltpu.VMEM((span, cols), f32),
            pltpu.VMEM((span, cols), f32),
            pltpu.VMEM((span, cols), f32),
            pltpu.VMEM((PAIRS * (rows // 8) * FLAT * PITCH, 2 * depth), f32),
            pltpu.VMEM((count * 4 * TY, 2 * depth), f32),
            pltpu.VMEM((count * 4 * TY, 2 * depth), f32),
            pltpu.VMEM(((2 * ngx + 2) * (ngy * TY + 16), 2 * depth), f32),
            pltpu.VMEM((4 * entries, 128), i32),
            pltpu.SMEM((4 * entries, 128), i32),
            pltpu.SemaphoreType.DMA,
        ],
        compiler_params=pltpu.CompilerParams(vmem_limit_bytes=LIMIT1),
        name="migrate",
    )(filter_taps, aperture.T, midpoint.T, traces, time_index.T, time_frac.T, amplitude.T)
    image = pl.pallas_call(
        functools.partial(exchange_kernel, count // 2),
        out_shape=jax.ShapeDtypeStruct((TX, TY * depth), jnp.float32),
        in_specs=[pl.BlockSpec(memory_space=pl.ANY)],
        out_specs=vmem,
        scratch_shapes=[
            *[pltpu.VMEM((count // 2, 2 * TY, 2 * depth), bf16)] * 4,
            *[pltpu.SemaphoreType.DMA] * 3,
            *[pltpu.SemaphoreType.DMA((count // 2,))] * 2,
        ],
        compiler_params=pltpu.CompilerParams(collective_id=0, has_side_effects=True, vmem_limit_bytes=LIMIT2),
        name="exchange",
    )(parts)
    return image


def solution(mesh):
    in_specs = (
        P(("gx", "gy"), None),
        P(),
        P(("gx", "gy"), None),
        P(("gx", "gy"), None),
        P(),
        P(),
        P(),
    )
    return jax.shard_map(
        functools.partial(body, mesh.shape["gx"], mesh.shape["gy"]),
        mesh=mesh,
        in_specs=in_specs,
        out_specs=P("gx", "gy"),
        check_vma=False,
    )
```
